512 devices in a mesh: side: 2 (over core), grp: 8 (over y), dev: 32 (over x, z).
Axes of the slice: x: 4, y: 8, z: 8, core: 2. Of those that a mesh axis runs over, the one named last changes fastest.
Arguments:
- tokens: bfloat16 [1024, 7168], P(('side', 'grp', 'dev')), may hold values from -6 to 6
- expert_ids: int32 [1024, 8], P(('side', 'grp', 'dev')), may hold values from 0 to 31, all different within a row; in each aligned block of 64 rows (0 to 63, 64 to 127, ...) at most 32 rows name the same one
- route_weights: bfloat16 [1024, 8], P(('side', 'grp', 'dev')), may hold values from 0.19921875 to 1.5
- w_gate: bfloat16 [32, 7168, 2048], P('dev', None, ('side', 'grp')), may hold values from -0.0625 to 0.0625
- w_down: bfloat16 [32, 2048, 7168], P('dev', None, ('side', 'grp')), may hold values from -0.125 to 0.125
Outputs:
- mixed: bfloat16 [1024, 7168], P(('side', 'grp', 'dev'))
The draws below stay inside these ranges and needn't reach their ends.
Inputs may be any that keep to these rules, and one draw needn't show every extreme that they name: `expert_ids`: each token names 8 different experts. In each aligned block of 64 tokens (the tokens of one group of devices along dev) no expert is named by more than 32 tokens, and in some block one expert is named by exactly 32.
All inputs are finite; a program needn't handle non-finite values.
Results may differ from the reference program's by a relative error of at most 0.0075.
Values may be sent and summed in bfloat16 or wider, within the bound.
No kernel may reach another device: no remote copies, remote signals or barrier semaphores. Data moves between devices by JAX's collectives and lax.ppermute only.
A program may use at most 64 MiB of HBM per device.

```python
import math
import jax
import jax.numpy as jnp
import numpy as np
from jax import lax

D = 7168
FF = 2048
TOPK = 8
ROWS_DEV = 2
EXPERTS = 32
CAP = 32
TOKENS = 1024
N_DEV = 32


def level_of(key, shape, cuts, smallest, largest):
    level = 1.0
    for dim, parts in cuts:
        steps = jax.random.uniform(jax.random.fold_in(jax.random.fold_in(key, 6), dim), (parts,), jnp.float32, smallest / len(cuts), largest / len(cuts))
        level = level * jnp.repeat(jnp.exp(steps), shape[dim] // parts).reshape((-1,) + (1,) * (len(shape) - 1 - dim))
    return level


def routed_block(own_key, own, number, rows, count, top, reach, slope):
    sequence = jax.random.permutation(own_key, count)
    packed, common = portions_of(count, rows * top, reach, slope, True), portions_of(count, rows * top, reach, slope, False)
    places = jnp.arange(count)

    def named(tallies, offset_by):
        used = int((tallies > 0).sum())
        fixed = max(1, used // 4)
        passed = fixed + (places - fixed + offset_by * (used - fixed)) % max(1, count - fixed)
        return jnp.zeros((count,), jnp.int32).at[sequence[jnp.where(places < fixed, places, passed)]].set(jnp.asarray(tallies, jnp.int32))

    tallies = jnp.where(number % 4 == 0, named(packed, number // 4), named(common, number - number // 4 - 1))
    mixed = jax.random.permutation(jax.random.fold_in(own, 3), count)
    giver, sink = mixed[0:count // 2 * 2:2], mixed[1:count // 2 * 2:2]
    slack = jnp.minimum(tallies[giver] - 1, reach - tallies[sink]) // 2
    slack = jnp.where((giver == sequence[0]) | (sink == sequence[0]) | (tallies[sink] == 0), 0, jnp.maximum(slack, 0))
    passed = jax.random.randint(jax.random.fold_in(own, 4), (count // 2,), 0, 1 << 20) % (slack + 1)
    tallies = tallies.at[giver].add(-passed).at[sink].add(passed)
    items = jnp.searchsorted(jnp.cumsum(tallies), jnp.arange(rows * top), side="right").astype(jnp.int32)
    table = items.reshape(top, rows).T
    table = table[jax.random.permutation(jax.random.fold_in(own, 1), rows)]
    offset_by = jax.random.randint(jax.random.fold_in(own, 2), (rows, 1), 0, top)
    return jnp.take_along_axis(table, (jnp.arange(top)[None, :] + offset_by) % top, axis=1)


def portions_of(count, total, most, skew, full):
    weights = [(1 << 20) // math.isqrt(grade ** skew) + 1 for grade in range(1, count + 1)]
    largest = most if full else min(most, max(-(-total // count), total * weights[0] // sum(weights)))
    least = 1 if total - largest >= count - 1 else 0
    counts, rest = [largest] + [least] * (count - 1), total - largest - least * (count - 1)
    while rest > 0:
        movable = [i for i in range(1, count) if counts[i] < largest] or [i for i in range(1, count) if counts[i] < most]
        pool, remaining = sum([weights[i] for i in movable]), rest
        for i in movable:
            more = min(most - counts[i], max(1, remaining * weights[i] // pool), rest)
            counts[i] = counts[i] + more
            rest = rest - more
    return np.array(counts)


def bell_draw(own_key, shape, deviation, limit, shards=(), held_as=jnp.bfloat16):
    drawn = jax.random.normal(own_key, shape, jnp.float32) * deviation
    if len(shards) > 0:
        drawn = level_of(own_key, shape, shards, -0.22, 0.18) * drawn
    return jnp.clip(drawn, min=-limit, max=limit).astype(held_as)


def setup_inputs(seed: int = 0) -> dict:
    key_of = jax.random.split(jax.random.key(seed), 6)
    tokens = bell_draw(key_of[0], (TOKENS, D), 1.0, 6.0, ((0, 512),))
    expert_ids_keys = jax.random.split(jax.random.fold_in(key_of[1], 1), TOKENS // (ROWS_DEV * N_DEV))
    expert_ids_turns = jax.random.permutation(jax.random.fold_in(key_of[1], 3), TOKENS // (ROWS_DEV * N_DEV))
    expert_ids = jax.vmap(lambda own, number: routed_block(jax.random.fold_in(key_of[1], 2), own, number, ROWS_DEV * N_DEV, EXPERTS, TOPK, CAP, 2))(expert_ids_keys, expert_ids_turns).reshape((TOKENS, TOPK))
    route_weights = jnp.clip(jnp.exp(math.log(1.5) - 2.018817 * jax.random.uniform(key_of[2], (TOKENS, TOPK), jnp.float32) ** level_of(key_of[2], (TOKENS, TOPK), ((0, 512),), -0.2, 0.2)), 0.19921875, 1.5).astype(jnp.bfloat16)
    w_gate = bell_draw(key_of[3], (EXPERTS, D, FF), D ** -0.5, 0.0625, ((0, 32), (2, 16)))
    w_down = bell_draw(key_of[4], (EXPERTS, FF, D), FF ** -0.5, 0.125, ((0, 32), (2, 16)))
    return {"tokens": tokens, "expert_ids": expert_ids, "route_weights": route_weights, "w_gate": w_gate, "w_down": w_down}


def rms_rows(tokens):
    values = tokens.astype(jnp.float32)
    scale = lax.rsqrt(lax.optimization_barrier(jnp.mean(values * values, axis=1, keepdims=True)) + 1e-06)
    return (values * scale).astype(jnp.bfloat16)

def reference(tokens, expert_ids, route_weights, w_gate, w_down):
    normed = rms_rows(tokens)
    total_rows = tokens.shape[0]
    group_size = ROWS_DEV * N_DEV
    groups = total_rows // group_size
    buffer = groups * CAP
    token_index = jnp.arange(total_rows, dtype=jnp.int32)
    group_of = token_index // group_size

    def one_expert(total, expert):
        match = expert_ids == expert
        hit = jnp.any(match, axis=1)
        hit_int = hit.astype(jnp.int32)
        rank = jnp.cumsum(hit_int.reshape(groups, group_size), axis=1).reshape(total_rows) - hit_int
        position = jnp.where(hit, group_of * CAP + rank, buffer).astype(jnp.int32)
        source = jnp.zeros((buffer,), jnp.int32).at[position].set(token_index, mode='drop')
        filled = jnp.zeros((buffer,), jnp.bool_).at[position].set(True, mode='drop')
        rows = jnp.where(filled[:, None], normed[source].astype(jnp.float32), jnp.float32(0.0))
        gate_matrix = lax.dynamic_index_in_dim(w_gate, expert, 0, keepdims=False).astype(jnp.float32)
        down_matrix = lax.dynamic_index_in_dim(w_down, expert, 0, keepdims=False).astype(jnp.float32)
        gate = jnp.dot(rows, gate_matrix, precision=lax.Precision.HIGHEST)
        hidden = lax.optimization_barrier(jax.nn.silu(gate).astype(jnp.bfloat16)).astype(jnp.float32)
        output = jnp.dot(hidden, down_matrix, precision=lax.Precision.HIGHEST).astype(jnp.bfloat16)
        weight = lax.optimization_barrier(jnp.sum(jnp.where(match, route_weights.astype(jnp.float32), jnp.float32(0.0)), axis=1))
        picked = output[jnp.minimum(position, buffer - 1)].astype(jnp.float32)
        total = total + jnp.where(hit[:, None], weight[:, None] * picked, jnp.float32(0.0))
        return (total, None)
    start = jnp.zeros((total_rows, tokens.shape[1]), jnp.float32)
    total, unused = lax.scan(one_expert, start, jnp.arange(EXPERTS, dtype=jnp.int32))
    return total.astype(jnp.bfloat16)
```

```python
import jax
import jax.numpy as jnp
from jax import lax
from jax.sharding import Mesh, PartitionSpec as P

CAP = 32
TOPK = 8
TAIL = 128


def rms_rows(tokens):
    values = tokens.astype(jnp.float32)
    scale = lax.rsqrt(jnp.mean(values * values, axis=1, keepdims=True) + 1e-06)
    return (values * scale).astype(jnp.bfloat16)


def side_by_side(own, side):
    other = lax.ppermute(own, "side", [(0, 1), (1, 0)])
    first = jnp.where(side == 0, own, other)
    second = jnp.where(side == 0, other, own)
    return jnp.concatenate([first, second], axis=1)


def on_device(tokens, expert_ids, route_weights, w_gate, w_down):
    bf16, f32, i32 = jnp.bfloat16, jnp.float32, jnp.int32
    rows, width = tokens.shape
    n_side, n_grp = lax.axis_size("side"), lax.axis_size("grp")
    n_x, n_z = lax.axis_size("x"), lax.axis_size("z")
    n_dev = n_x * n_z
    side = lax.axis_index("side")
    dev = lax.axis_index("x") * n_z + lax.axis_index("z")
    unit = w_gate.shape[2]

    gate_slab = jnp.pad(side_by_side(w_gate[0], side), ((0, TAIL), (0, 0)))
    down_slab = side_by_side(w_down[0], side)
    down_slab = (
        down_slab.reshape(n_side, n_grp, unit, -1)
        .transpose(1, 0, 2, 3)
        .reshape(n_side * n_grp * unit, -1)
    )

    place = (dev * rows + jnp.arange(rows, dtype=i32)).astype(bf16)
    tail = jnp.concatenate([expert_ids.astype(bf16), route_weights, place[:, None]], axis=1)
    sent = jnp.concatenate(
        [rms_rows(tokens), jnp.pad(tail, ((0, 0), (0, TAIL - 2 * TOPK - 1)))], axis=1
    )
    by_z = lax.all_to_all(
        jnp.broadcast_to(sent[None], (n_z,) + sent.shape), "z", split_axis=0, concat_axis=0, tiled=True
    ).reshape(n_z * rows, -1)
    packed = lax.all_gather(by_z, "x", axis=0, tiled=True)

    group = n_dev * rows
    hit = jnp.any(packed[:, width : width + TOPK].astype(i32) == dev, axis=1)
    before = jnp.arange(group)[:, None] < jnp.arange(group)[None, :]
    slot = jnp.sum((before & hit[:, None]).astype(i32), axis=0)
    placed = (slot[None, :] == jnp.arange(CAP, dtype=i32)[:, None]) & hit[None, :]
    slot_input = jnp.dot(placed.astype(bf16), packed, preferred_element_type=f32).astype(bf16)
    inputs = lax.all_gather(slot_input, "grp", axis=0, tiled=True)

    hidden = jax.nn.silu(jnp.dot(inputs, gate_slab, preferred_element_type=f32)).astype(bf16)
    columns = jnp.dot(
        lax.all_gather(hidden, "grp", axis=1, tiled=True), down_slab, preferred_element_type=f32
    ).astype(bf16)

    slots = n_grp * CAP
    notes = inputs[:, width:]
    ids = notes[:, :TOPK].astype(i32)
    weight = jnp.sum(
        jnp.where(ids == dev, notes[:, TOPK : 2 * TOPK].astype(f32), 0.0), axis=1
    ).astype(bf16)
    place = notes[:, 2 * TOPK].astype(i32)
    of_group = jnp.arange(slots, dtype=i32) // CAP
    target = (place // rows) * (n_grp * rows) + of_group * rows + place % rows
    combine = jnp.where(
        jnp.arange(n_grp * group, dtype=i32)[:, None] == target[None, :],
        weight[None, :],
        jnp.zeros((), bf16),
    )
    weighted = jnp.dot(combine, columns, preferred_element_type=f32).astype(bf16)
    over_x = lax.all_to_all(
        weighted.reshape(n_x, n_z * n_grp * rows, -1), "x", split_axis=0, concat_axis=0, tiled=True
    )
    total_x = jnp.sum(over_x.astype(f32), axis=0).astype(bf16)
    over_zy = lax.all_to_all(
        total_x.reshape(n_z * n_grp, rows, -1), ("z", "grp"), split_axis=0, concat_axis=0, tiled=True
    )
    total = jnp.sum(over_zy.reshape(n_z, n_grp, rows, -1).astype(f32), axis=0).astype(bf16)
    mixed = total.reshape(n_grp, rows, n_side, -1).transpose(1, 2, 0, 3)
    return mixed.reshape(rows, width)


def solution(mesh):
    side, grp, dev = mesh.devices.shape
    n_z = 8
    fine = Mesh(mesh.devices.reshape(side, grp, dev // n_z, n_z), ("side", "grp", "x", "z"))
    row_axes = ("side", "grp", "x", "z")
    in_specs = (
        P(row_axes, None),
        P(row_axes, None),
        P(row_axes, None),
        P(("x", "z"), None, ("side", "grp")),
        P(("x", "z"), None, ("side", "grp")),
    )
    return jax.shard_map(
        on_device, mesh=fine, in_specs=in_specs, out_specs=P(row_axes, None), check_vma=False
    )
```

```python
import functools

import jax
import jax.numpy as jnp
from jax import lax
from jax.experimental import pallas as pl
from jax.experimental.pallas import tpu as pltpu
from jax.sharding import Mesh, PartitionSpec as P

CAP = 32
TOPK = 8
TAIL = 128
SHIFT = 64
SPOT = 32


def rms_rows(tokens):
    values = tokens.astype(jnp.float32)
    scale = lax.rsqrt(jnp.mean(values * values, axis=1, keepdims=True) + 1e-06)
    return (values * scale).astype(jnp.bfloat16)


def side_by_side(own, side, axis):
    other = lax.ppermute(own, "side", [(0, 1), (1, 0)])
    first = jnp.where(side == 0, own, other)
    second = jnp.where(side == 0, other, own)
    return jnp.concatenate([first, second], axis=axis)


def down_kernel(n_grp, n_side, unit, rows, near, where_ref, near_ref, far_ref, slab_ref, *refs):
    *tails, out_ref, hidden_ref, notes_ref = refs
    grp, dev = where_ref[0], where_ref[1]
    for g in range(n_grp):
        for j in range(n_grp):
            d = (j - g) % n_grp
            for k in range(n_side):
                units = slice(k * unit, (k + 1) * unit)
                if d in near:
                    start = near.index(d) * CAP
                    block = near_ref[g, start : start + CAP, units]
                else:
                    block = far_ref[g, :, units]
                at = (k * n_grp + g) * unit
                hidden_ref[j * CAP : (j + 1) * CAP, at : at + unit] = block
    for d in range(n_grp):
        j = lax.rem(grp + d, n_grp)
        notes_ref[pl.ds(pl.multiple_of(j * CAP, CAP), CAP), :] = tails[d][...]
    columns = lax.dot_general(
        hidden_ref[...], slab_ref[...], (((1,), (1,)), ((), ())), preferred_element_type=jnp.float32
    ).astype(jnp.bfloat16)
    slots, tokens = hidden_ref.shape[0], out_ref.shape[0]
    notes = notes_ref[...].astype(jnp.float32)
    lane = lax.broadcasted_iota(jnp.int32, notes.shape, 1)
    mine = (lane < TOPK) & (notes.astype(jnp.int32) == dev)
    weight = jnp.sum(jnp.where(mine, pltpu.roll(notes, SHIFT, 1), 0.0), axis=1, keepdims=True)
    place = jnp.sum(jnp.where(lane == SPOT, notes, 0.0), axis=1, keepdims=True).astype(jnp.int32)
    shift = rows.bit_length() - 1
    of_group = lax.broadcasted_iota(jnp.int32, (slots, 1), 0) // CAP
    target = (place >> shift) * (n_grp * rows) + of_group * rows + (place & (rows - 1))
    combine = jnp.where(
        lax.broadcasted_iota(jnp.int32, (slots, tokens), 1) == target, weight, 0.0
    ).astype(jnp.bfloat16)
    out_ref[...] = lax.dot_general(
        combine, columns, (((0,), (0,)), ((), ())), preferred_element_type=jnp.float32
    ).astype(jnp.bfloat16)


def on_device(tokens, expert_ids, route_weights, w_gate, w_down):
    bf16, f32, i32 = jnp.bfloat16, jnp.float32, jnp.int32
    rows, width = tokens.shape
    n_side, n_grp = lax.axis_size("side"), lax.axis_size("grp")
    n_x, n_z = lax.axis_size("x"), lax.axis_size("z")
    n_dev = n_x * n_z
    side = lax.axis_index("side")
    dev = lax.axis_index("x") * n_z + lax.axis_index("z")
    unit = w_gate.shape[2]

    gate_slab = jnp.pad(side_by_side(w_gate[0], side, 1), ((0, TAIL), (0, 0)))
    down_slab = side_by_side(w_down[0].T, side, 0)

    place = (dev * rows + jnp.arange(rows, dtype=i32)).astype(bf16)
    tail = jnp.concatenate(
        [
            jnp.pad(expert_ids.astype(bf16), ((0, 0), (0, SPOT - TOPK))),
            jnp.pad(place[:, None], ((0, 0), (0, SHIFT - SPOT - 1))),
            jnp.pad(route_weights, ((0, 0), (0, TAIL - SHIFT - TOPK))),
        ],
        axis=1,
    )
    sent = jnp.concatenate([rms_rows(tokens), tail], axis=1)
    by_z = lax.all_to_all(
        jnp.broadcast_to(sent[None], (n_z,) + sent.shape), "z", split_axis=0, concat_axis=0, tiled=True
    ).reshape(n_z * rows, -1)
    packed = lax.all_gather(by_z, "x", axis=0, tiled=True)

    group = n_dev * rows
    hit = jnp.any(packed[:, width : width + TOPK].astype(i32) == dev, axis=1)
    before = jnp.arange(group)[:, None] < jnp.arange(group)[None, :]
    slot = jnp.sum((before & hit[:, None]).astype(i32), axis=0)
    placed = (slot[None, :] == jnp.arange(CAP, dtype=i32)[:, None]) & hit[None, :]
    slot_input = jnp.dot(placed.astype(bf16), packed, preferred_element_type=f32).astype(bf16)

    def silu_gate(block):
        return jax.nn.silu(jnp.dot(block, gate_slab, preferred_element_type=f32)).astype(bf16)

    up = [(i, (i + 1) % n_grp) for i in range(n_grp)]
    down = [(i, (i - 1) % n_grp) for i in range(n_grp)]
    half = CAP // 2
    blocks = {0: slot_input}
    hidden = [silu_gate(slot_input)]
    near = [0]
    below = above = slot_input
    for step in range(1, n_grp // 2):
        below = lax.ppermute(below, "grp", up)
        above = lax.ppermute(above, "grp", down)
        blocks[n_grp - step], blocks[step] = below, above
        near += [n_grp - step, step]
        hidden.append(silu_gate(jnp.concatenate([below, above], axis=0)))
    last = [lax.ppermute(below[:half], "grp", up), lax.ppermute(above[half:], "grp", down)]
    got_near = lax.all_gather(jnp.concatenate(hidden, axis=0), "grp", axis=0, tiled=True)
    got_near, *last = lax.optimization_barrier((got_near, *last))
    far = n_grp // 2
    blocks[far] = jnp.concatenate(last, axis=0)
    hidden_far = silu_gate(blocks[far])
    got_far = lax.all_to_all(
        jnp.broadcast_to(hidden_far[None], (n_grp,) + hidden_far.shape),
        "grp",
        split_axis=0,
        concat_axis=0,
        tiled=True,
    )
    slots = n_grp * CAP
    weighted = pl.pallas_call(
        functools.partial(down_kernel, n_grp, n_side, unit, rows, near),
        out_shape=jax.ShapeDtypeStruct((n_grp * group, down_slab.shape[0]), bf16),
        in_specs=[pl.BlockSpec(memory_space=pltpu.SMEM)]
        + [pl.BlockSpec(memory_space=pltpu.VMEM)] * (3 + n_grp),
        out_specs=pl.BlockSpec(memory_space=pltpu.VMEM),
        scratch_shapes=[
            pltpu.VMEM((slots, down_slab.shape[1]), bf16),
            pltpu.VMEM((slots, TAIL), bf16),
        ],
        compiler_params=pltpu.CompilerParams(vmem_limit_bytes=40 * 2**20),
    )(
        jnp.stack([lax.axis_index("grp"), dev]).astype(i32),
        got_near.reshape(n_grp, len(near) * CAP, -1),
        got_far,
        down_slab,
        *[blocks[d][:, width:] for d in range(n_grp)],
    )
    parts = lax.all_to_all(
        weighted.reshape(n_dev * n_grp, rows, -1), ("x", "z", "grp"), split_axis=0, concat_axis=0, tiled=True
    )
    total = jnp.sum(parts.reshape(n_dev, n_grp, rows, -1).astype(f32), axis=0).astype(bf16)
    mixed = total.reshape(n_grp, rows, n_side, -1).transpose(1, 2, 0, 3)
    return mixed.reshape(rows, width)


def solution(mesh):
    side, grp, dev = mesh.devices.shape
    n_z = 8
    fine = Mesh(mesh.devices.reshape(side, grp, dev // n_z, n_z), ("side", "grp", "x", "z"))
    row_axes = ("side", "grp", "x", "z")
    in_specs = (
        P(row_axes, None),
        P(row_axes, None),
        P(row_axes, None),
        P(("x", "z"), None, ("side", "grp")),
        P(("x", "z"), None, ("side", "grp")),
    )
    return jax.shard_map(
        on_device, mesh=fine, in_specs=in_specs, out_specs=P(row_axes, None), check_vma=False
    )
```

```python
import functools

import jax
import jax.numpy as jnp
from jax import lax
from jax.experimental import pallas as pl
from jax.experimental.pallas import tpu as pltpu
from jax.sharding import Mesh, PartitionSpec as P

CAP = 32
TOPK = 8
TAIL = 128
SHIFT = 64
SPOT = 32


def send_kernel(rows, dev_ref, tokens_ref, ids_ref, weights_ref, out_ref):
    values = tokens_ref[...].astype(jnp.float32)
    width = values.shape[1]
    scale = lax.rsqrt(jnp.mean(values * values, axis=1, keepdims=True) + 1e-06)
    normed = (values * scale).astype(jnp.bfloat16)
    ids, weights = ids_ref[...].astype(jnp.float32), weights_ref[...].astype(jnp.float32)
    lane = lax.broadcasted_iota(jnp.int32, (rows, TAIL), 1)
    place = (dev_ref[0] * rows + lax.broadcasted_iota(jnp.int32, (rows, TAIL), 0)).astype(jnp.float32)
    tail = jnp.where(lane == SPOT, place, 0.0)
    for k in range(TOPK):
        tail = jnp.where(lane == k, ids[:, k : k + 1], tail)
        tail = jnp.where(lane == SHIFT + k, weights[:, k : k + 1], tail)
    tail = tail.astype(jnp.bfloat16)
    for z in range(out_ref.shape[0]):
        out_ref[z, :, :width] = normed
        out_ref[z, :, width:] = tail


def from_other_core(own):
    return lax.ppermute(own, "side", [(0, 1), (1, 0)])


def down_kernel(n_grp, n_side, unit, rows, order, where_ref, own_ref, other_ref, *refs):
    got, tails = refs[: len(order)], refs[len(order) : len(order) + n_grp]
    out_ref, hidden_ref, notes_ref, slab_ref, sems = refs[len(order) + n_grp :]
    grp, dev, side = where_ref[0], where_ref[1], where_ref[2]
    width = own_ref.shape[0]
    copies = [
        pltpu.make_async_copy(own_ref, slab_ref.at[pl.ds(pl.multiple_of(side * width, 64), width)], sems.at[0]),
        pltpu.make_async_copy(
            other_ref, slab_ref.at[pl.ds(pl.multiple_of((1 - side) * width, 64), width)], sems.at[1]
        ),
    ]
    for copy in copies:
        copy.start()
    for g in range(n_grp):
        for j in range(n_grp):
            d = (j - g) % n_grp
            for ref, distances in zip(got, order):
                if d in distances:
                    start = distances.index(d) * CAP
                    for k in range(n_side):
                        at = (k * n_grp + g) * unit
                        hidden_ref[j * CAP : (j + 1) * CAP, at : at + unit] = ref[
                            g, start : start + CAP, k * unit : (k + 1) * unit
                        ]
    for d in range(n_grp):
        j = lax.rem(grp + d, n_grp)
        notes_ref[pl.ds(pl.multiple_of(j * CAP, CAP), CAP), :] = tails[d][...]
    for copy in copies:
        copy.wait()
    columns = lax.dot_general(
        hidden_ref[...], slab_ref[...], (((1,), (1,)), ((), ())), preferred_element_type=jnp.float32
    ).astype(jnp.bfloat16)
    slots, tokens = hidden_ref.shape[0], out_ref.shape[0]
    notes = notes_ref[...].astype(jnp.float32)
    lane = lax.broadcasted_iota(jnp.int32, notes.shape, 1)
    mine = (lane < TOPK) & (notes.astype(jnp.int32) == dev)
    weight = jnp.sum(jnp.where(mine, pltpu.roll(notes, SHIFT, 1), 0.0), axis=1, keepdims=True)
    place = jnp.sum(jnp.where(lane == SPOT, notes, 0.0), axis=1, keepdims=True).astype(jnp.int32)
    shift = rows.bit_length() - 1
    of_group = lax.broadcasted_iota(jnp.int32, (slots, 1), 0) // CAP
    target = (place >> shift) * (n_grp * rows) + of_group * rows + (place & (rows - 1))
    combine = jnp.where(
        lax.broadcasted_iota(jnp.int32, (slots, tokens), 1) == target, weight, 0.0
    ).astype(jnp.bfloat16)
    out_ref[...] = lax.dot_general(
        combine, columns, (((0,), (0,)), ((), ())), preferred_element_type=jnp.float32
    ).astype(jnp.bfloat16)


def on_device(tokens, expert_ids, route_weights, w_gate, w_down):
    bf16, f32, i32 = jnp.bfloat16, jnp.float32, jnp.int32
    rows, width = tokens.shape
    n_side, n_grp = lax.axis_size("side"), lax.axis_size("grp")
    n_x, n_z = lax.axis_size("x"), lax.axis_size("z")
    n_dev = n_x * n_z
    side = lax.axis_index("side")
    dev = lax.axis_index("x") * n_z + lax.axis_index("z")
    unit = w_gate.shape[2]

    own_gate, own_down = w_gate[0], w_down[0].T
    other_gate, other_down = from_other_core(own_gate), from_other_core(own_down)

    vmem, smem = pl.BlockSpec(memory_space=pltpu.VMEM), pl.BlockSpec(memory_space=pltpu.SMEM)
    copies = pl.pallas_call(
        functools.partial(send_kernel, rows),
        out_shape=jax.ShapeDtypeStruct((n_z, rows, width + TAIL), bf16),
        in_specs=[smem, vmem, vmem, vmem],
        out_specs=vmem,
    )(dev.reshape(1).astype(i32), tokens, expert_ids, route_weights)
    by_z = lax.all_to_all(copies, "z", split_axis=0, concat_axis=0, tiled=True).reshape(n_z * rows, -1)
    packed = lax.all_gather(by_z, "x", axis=0, tiled=True)

    group = n_dev * rows
    hit = jnp.any(packed[:, width : width + TOPK].astype(i32) == dev, axis=1)
    before = jnp.arange(group)[:, None] < jnp.arange(group)[None, :]
    slot = jnp.sum((before & hit[:, None]).astype(i32), axis=0)
    placed = (slot[None, :] == jnp.arange(CAP, dtype=i32)[:, None]) & hit[None, :]
    slot_input = jnp.dot(placed.astype(bf16), packed, preferred_element_type=f32).astype(bf16)

    gate_slab = jnp.pad(
        jnp.concatenate(
            [jnp.where(side == 0, own_gate, other_gate), jnp.where(side == 0, other_gate, own_gate)], axis=1
        ),
        ((0, TAIL), (0, 0)),
    )

    def silu_gate(block):
        return jax.nn.silu(jnp.dot(block, gate_slab, preferred_element_type=f32)).astype(bf16)

    def to_all(hidden):
        return lax.all_to_all(
            jnp.broadcast_to(hidden[None], (n_grp,) + hidden.shape), "grp", split_axis=0, concat_axis=0, tiled=True
        )

    up = [(i, (i + 1) % n_grp) for i in range(n_grp)]
    down = [(i, (i - 1) % n_grp) for i in range(n_grp)]
    half, far = CAP // 2, n_grp // 2
    blocks = {0: slot_input}
    below = above = held = slot_input
    hidden, order = [[], []], [[], []]
    distances = [0]
    got_early = None
    for step in range(1, far + 1):
        if step < far:
            below = lax.ppermute(below, "grp", up)
            above = lax.ppermute(above, "grp", down)
        else:
            below, above = lax.ppermute(below[:half], "grp", up), lax.ppermute(above[half:], "grp", down)
        part = 0 if step <= far - 1 else 1
        hidden[part].append(silu_gate(held))
        order[part] += distances
        below, above, hidden[part][-1] = lax.optimization_barrier((below, above, hidden[part][-1]))
        if step == far - 1:
            got_early = to_all(jnp.concatenate(hidden[0], axis=0))
        held = jnp.concatenate([below, above], axis=0)
        distances = [far] if step == far else [n_grp - step, step]
        if step < far:
            blocks[n_grp - step], blocks[step] = below, above
    blocks[far] = held
    hidden[1].append(silu_gate(held))
    order[1] += distances
    got_late = to_all(jnp.concatenate(hidden[1], axis=0))

    slots = n_grp * CAP
    columns = n_side * own_down.shape[0]
    any_memory = pl.BlockSpec(memory_space=pl.ANY)
    weighted = pl.pallas_call(
        functools.partial(down_kernel, n_grp, n_side, unit, rows, order),
        out_shape=jax.ShapeDtypeStruct((n_grp * group, columns), bf16),
        in_specs=[smem, any_memory, any_memory] + [vmem] * (len(order) + n_grp),
        out_specs=vmem,
        scratch_shapes=[
            pltpu.VMEM((slots, own_down.shape[1]), bf16),
            pltpu.VMEM((slots, TAIL), bf16),
            pltpu.VMEM((columns, own_down.shape[1]), bf16),
            pltpu.SemaphoreType.DMA((2,)),
        ],
        compiler_params=pltpu.CompilerParams(vmem_limit_bytes=40 * 2**20),
    )(
        jnp.stack([lax.axis_index("grp"), dev, side]).astype(i32),
        own_down,
        other_down,
        got_early,
        got_late,
        *[blocks[d][:, width:] for d in range(n_grp)],
    )
    parts = lax.all_to_all(
        weighted.reshape(n_dev * n_grp, rows, -1), ("x", "z", "grp"), split_axis=0, concat_axis=0, tiled=True
    )
    total = jnp.sum(parts.reshape(n_dev, n_grp, rows, -1).astype(f32), axis=0).astype(bf16)
    mixed = total.reshape(n_grp, rows, n_side, -1).transpose(1, 2, 0, 3)
    return mixed.reshape(rows, width)


def solution(mesh):
    side, grp, dev = mesh.devices.shape
    n_z = 8
    fine = Mesh(mesh.devices.reshape(side, grp, dev // n_z, n_z), ("side", "grp", "x", "z"))
    row_axes = ("side", "grp", "x", "z")
    in_specs = (
        P(row_axes, None),
        P(row_axes, None),
        P(row_axes, None),
        P(("x", "z"), None, ("side", "grp")),
        P(("x", "z"), None, ("side", "grp")),
    )
    return jax.shard_map(
        on_device, mesh=fine, in_specs=in_specs, out_specs=P(row_axes, None), check_vma=False
    )
```

```python
import functools

import jax
import jax.numpy as jnp
from jax import lax
from jax.experimental import pallas as pl
from jax.experimental.pallas import tpu as pltpu
from jax.sharding import Mesh, PartitionSpec as P

CAP = 32
TOPK = 8
TAIL = 128
SHIFT = 64
SPOT = 32


def send_kernel(rows, dev_ref, tokens_ref, ids_ref, weights_ref, out_ref):
    values = tokens_ref[...].astype(jnp.float32)
    width = values.shape[1]
    scale = lax.rsqrt(jnp.mean(values * values, axis=1, keepdims=True) + 1e-06)
    normed = (values * scale).astype(jnp.bfloat16)
    ids, weights = ids_ref[...].astype(jnp.float32), weights_ref[...].astype(jnp.float32)
    lane = lax.broadcasted_iota(jnp.int32, (rows, TAIL), 1)
    place = (dev_ref[0] * rows + lax.broadcasted_iota(jnp.int32, (rows, TAIL), 0)).astype(jnp.float32)
    tail = jnp.where(lane == SPOT, place, 0.0)
    for k in range(TOPK):
        tail = jnp.where(lane == k, ids[:, k : k + 1], tail)
        tail = jnp.where(lane == SHIFT + k, weights[:, k : k + 1], tail)
    tail = tail.astype(jnp.bfloat16)
    for z in range(out_ref.shape[0]):
        out_ref[z, :, :width] = normed
        out_ref[z, :, width:] = tail


def from_other_core(own):
    return lax.ppermute(own, "side", [(0, 1), (1, 0)])


def down_kernel(n_grp, n_side, unit, rows, order, where_ref, own_ref, other_ref, *refs):
    got, tails = refs[: len(order)], refs[len(order) : len(order) + n_grp]
    out_ref, hidden_ref, notes_ref = refs[len(order) + n_grp :]
    grp, dev, side = where_ref[0], where_ref[1], where_ref[2]
    for g in range(n_grp):
        for j in range(n_grp):
            d = (j - g) % n_grp
            for ref, distances in zip(got, order):
                if d in distances:
                    start = distances.index(d) * CAP
                    for k in range(n_side):
                        at = (k * n_grp + g) * unit
                        hidden_ref[j * CAP : (j + 1) * CAP, at : at + unit] = ref[
                            g, start : start + CAP, k * unit : (k + 1) * unit
                        ]
    for d in range(n_grp):
        j = lax.rem(grp + d, n_grp)
        notes_ref[pl.ds(pl.multiple_of(j * CAP, CAP), CAP), :] = tails[d][...]
    own, other = [
        lax.dot_general(
            hidden_ref[...], slab[...], (((1,), (1,)), ((), ())), preferred_element_type=jnp.float32
        )
        for slab in (own_ref, other_ref)
    ]
    columns = [jnp.where(side == 0, own, other), jnp.where(side == 0, other, own)]
    slots, tokens = hidden_ref.shape[0], out_ref.shape[0]
    notes = notes_ref[...].astype(jnp.float32)
    lane = lax.broadcasted_iota(jnp.int32, notes.shape, 1)
    mine = (lane < TOPK) & (notes.astype(jnp.int32) == dev)
    weight = jnp.sum(jnp.where(mine, pltpu.roll(notes, SHIFT, 1), 0.0), axis=1, keepdims=True)
    place = jnp.sum(jnp.where(lane == SPOT, notes, 0.0), axis=1, keepdims=True).astype(jnp.int32)
    shift = rows.bit_length() - 1
    of_group = lax.broadcasted_iota(jnp.int32, (slots, 1), 0) // CAP
    target = (place >> shift) * (n_grp * rows) + of_group * rows + (place & (rows - 1))
    combine = jnp.where(
        lax.broadcasted_iota(jnp.int32, (slots, tokens), 1) == target, weight, 0.0
    ).astype(jnp.bfloat16)
    width = own_ref.shape[0]
    for k in range(n_side):
        out_ref[:, k * width : (k + 1) * width] = lax.dot_general(
            combine, columns[k].astype(jnp.bfloat16), (((0,), (0,)), ((), ())), preferred_element_type=jnp.float32
        ).astype(jnp.bfloat16)


def on_device(tokens, expert_ids, route_weights, w_gate, w_down):
    bf16, f32, i32 = jnp.bfloat16, jnp.float32, jnp.int32
    rows, width = tokens.shape
    n_side, n_grp = lax.axis_size("side"), lax.axis_size("grp")
    n_x, n_z = lax.axis_size("x"), lax.axis_size("z")
    n_dev = n_x * n_z
    side = lax.axis_index("side")
    dev = lax.axis_index("x") * n_z + lax.axis_index("z")
    unit = w_gate.shape[2]

    own_gate, own_down = w_gate[0], w_down[0].T
    other_down = from_other_core(own_down)

    vmem, smem = pl.BlockSpec(memory_space=pltpu.VMEM), pl.BlockSpec(memory_space=pltpu.SMEM)
    copies = pl.pallas_call(
        functools.partial(send_kernel, rows),
        out_shape=jax.ShapeDtypeStruct((n_z, rows, width + TAIL), bf16),
        in_specs=[smem, vmem, vmem, vmem],
        out_specs=vmem,
    )(dev.reshape(1).astype(i32), tokens, expert_ids, route_weights)
    own_gate, copies = lax.optimization_barrier((own_gate, copies))
    other_gate = from_other_core(own_gate)
    by_z = lax.all_to_all(copies, "z", split_axis=0, concat_axis=0, tiled=True).reshape(n_z * rows, -1)
    packed = lax.all_gather(by_z, "x", axis=0, tiled=True)

    group = n_dev * rows
    hit = jnp.any(packed[:, width : width + TOPK].astype(i32) == dev, axis=1)
    before = jnp.arange(group)[:, None] < jnp.arange(group)[None, :]
    slot = jnp.sum((before & hit[:, None]).astype(i32), axis=0)
    placed = (slot[None, :] == jnp.arange(CAP, dtype=i32)[:, None]) & hit[None, :]
    slot_input = jnp.dot(placed.astype(bf16), packed, preferred_element_type=f32).astype(bf16)

    gate_slab = jnp.pad(
        jnp.concatenate(
            [jnp.where(side == 0, own_gate, other_gate), jnp.where(side == 0, other_gate, own_gate)], axis=1
        ),
        ((0, TAIL), (0, 0)),
    )

    def silu_gate(block):
        return jax.nn.silu(jnp.dot(block, gate_slab, preferred_element_type=f32)).astype(bf16)

    def to_all(hidden):
        return lax.all_to_all(
            jnp.broadcast_to(hidden[None], (n_grp,) + hidden.shape), "grp", split_axis=0, concat_axis=0, tiled=True
        )

    up = [(i, (i + 1) % n_grp) for i in range(n_grp)]
    down = [(i, (i - 1) % n_grp) for i in range(n_grp)]
    half, far = CAP // 2, n_grp // 2
    blocks = {0: slot_input}
    below = above = held = slot_input
    hidden, order = [[], []], [[], []]
    distances = [0]
    got_early = None
    for step in range(1, far + 1):
        if step < far:
            below = lax.ppermute(below, "grp", up)
            above = lax.ppermute(above, "grp", down)
        else:
            below, above = lax.ppermute(below[:half], "grp", up), lax.ppermute(above[half:], "grp", down)
        product = silu_gate(held)
        part = 0 if step < far else 1
        hidden[part].append(product)
        order[part] += distances
        if step == far - 1:
            got_early = to_all(jnp.concatenate(hidden[0], axis=0))
        if step < far:
            below, product = lax.optimization_barrier((below, product))
        else:
            below, product, got_early = lax.optimization_barrier((below, product, got_early))
        hidden[part][-1] = product
        held = jnp.concatenate([below, above], axis=0)
        distances = [far] if step == far else [n_grp - step, step]
        if step < far:
            blocks[n_grp - step], blocks[step] = below, above
    blocks[far] = held
    hidden[1].append(silu_gate(held))
    order[1] += distances
    got_late = to_all(jnp.concatenate(hidden[1], axis=0))

    slots = n_grp * CAP
    columns = n_side * own_down.shape[0]
    weighted = pl.pallas_call(
        functools.partial(down_kernel, n_grp, n_side, unit, rows, order),
        out_shape=jax.ShapeDtypeStruct((n_grp * group, columns), bf16),
        in_specs=[smem] + [vmem] * (2 + len(order) + n_grp),
        out_specs=vmem,
        scratch_shapes=[
            pltpu.VMEM((slots, own_down.shape[1]), bf16),
            pltpu.VMEM((slots, TAIL), bf16),
        ],
        compiler_params=pltpu.CompilerParams(vmem_limit_bytes=40 * 2**20),
    )(
        jnp.stack([lax.axis_index("grp"), dev, side]).astype(i32),
        own_down,
        other_down,
        got_early,
        got_late,
        *[blocks[d][:, width:] for d in range(n_grp)],
    )
    parts = lax.all_to_all(
        weighted.reshape(n_dev * n_grp, rows, -1), ("x", "z", "grp"), split_axis=0, concat_axis=0, tiled=True
    )
    total = jnp.sum(parts.reshape(n_dev, n_grp, rows, -1).astype(f32), axis=0).astype(bf16)
    mixed = total.reshape(n_grp, rows, n_side, -1).transpose(1, 2, 0, 3)
    return mixed.reshape(rows, width)


def solution(mesh):
    side, grp, dev = mesh.devices.shape
    n_z = 8
    fine = Mesh(mesh.devices.reshape(side, grp, dev // n_z, n_z), ("side", "grp", "x", "z"))
    row_axes = ("side", "grp", "x", "z")
    in_specs = (
        P(row_axes, None),
        P(row_axes, None),
        P(row_axes, None),
        P(("x", "z"), None, ("side", "grp")),
        P(("x", "z"), None, ("side", "grp")),
    )
    return jax.shard_map(
        on_device, mesh=fine, in_specs=in_specs, out_specs=P(row_axes, None), check_vma=False
    )
```

```python
import functools

import jax
import jax.numpy as jnp
from jax import lax
from jax.experimental import pallas as pl
from jax.experimental.pallas import tpu as pltpu
from jax.sharding import Mesh, PartitionSpec as P

CAP = 32
TOPK = 8
TAIL = 128
SHIFT = 64
SPOT = 32


def send_kernel(rows, dev_ref, tokens_ref, ids_ref, weights_ref, out_ref):
    values = tokens_ref[...].astype(jnp.float32)
    width = values.shape[1]
    scale = lax.rsqrt(jnp.mean(values * values, axis=1, keepdims=True) + 1e-06)
    normed = (values * scale).astype(jnp.bfloat16)
    ids, weights = ids_ref[...].astype(jnp.float32), weights_ref[...].astype(jnp.float32)
    lane = lax.broadcasted_iota(jnp.int32, (rows, TAIL), 1)
    place = (dev_ref[0] * rows + lax.broadcasted_iota(jnp.int32, (rows, TAIL), 0)).astype(jnp.float32)
    tail = jnp.where(lane == SPOT, place, 0.0)
    for k in range(TOPK):
        tail = jnp.where(lane == k, ids[:, k : k + 1], tail)
        tail = jnp.where(lane == SHIFT + k, weights[:, k : k + 1], tail)
    tail = tail.astype(jnp.bfloat16)
    for z in range(out_ref.shape[0]):
        out_ref[z, :, :width] = normed
        out_ref[z, :, width:] = tail


def from_other_core(own):
    return lax.ppermute(own, "side", [(0, 1), (1, 0)])


def down_kernel(n_grp, n_side, unit, rows, order, where_ref, own_ref, other_ref, got_ref, *refs):
    *tails, out_ref, hidden_ref, notes_ref = refs
    grp, dev, side = where_ref[0], where_ref[1], where_ref[2]
    for g in range(n_grp):
        for j in range(n_grp):
            start = order.index((j - g) % n_grp) * CAP
            for k in range(n_side):
                at = (k * n_grp + g) * unit
                hidden_ref[j * CAP : (j + 1) * CAP, at : at + unit] = got_ref[
                    g, start : start + CAP, k * unit : (k + 1) * unit
                ]
    for d in range(n_grp):
        j = lax.rem(grp + d, n_grp)
        notes_ref[pl.ds(pl.multiple_of(j * CAP, CAP), CAP), :] = tails[d][...]
    own, other = [
        lax.dot_general(
            hidden_ref[...], slab[...], (((1,), (1,)), ((), ())), preferred_element_type=jnp.float32
        )
        for slab in (own_ref, other_ref)
    ]
    columns = [jnp.where(side == 0, own, other), jnp.where(side == 0, other, own)]
    slots, tokens = hidden_ref.shape[0], out_ref.shape[0]
    notes = notes_ref[...].astype(jnp.float32)
    lane = lax.broadcasted_iota(jnp.int32, notes.shape, 1)
    mine = (lane < TOPK) & (notes.astype(jnp.int32) == dev)
    weight = jnp.sum(jnp.where(mine, pltpu.roll(notes, SHIFT, 1), 0.0), axis=1, keepdims=True)
    place = jnp.sum(jnp.where(lane == SPOT, notes, 0.0), axis=1, keepdims=True).astype(jnp.int32)
    shift = rows.bit_length() - 1
    of_group = lax.broadcasted_iota(jnp.int32, (slots, 1), 0) // CAP
    target = (place >> shift) * (n_grp * rows) + of_group * rows + (place & (rows - 1))
    combine = jnp.where(
        lax.broadcasted_iota(jnp.int32, (slots, tokens), 1) == target, weight, 0.0
    ).astype(jnp.bfloat16)
    width = own_ref.shape[0]
    for k in range(n_side):
        out_ref[:, k * width : (k + 1) * width] = lax.dot_general(
            combine, columns[k].astype(jnp.bfloat16), (((0,), (0,)), ((), ())), preferred_element_type=jnp.float32
        ).astype(jnp.bfloat16)


def on_device(tokens, expert_ids, route_weights, w_gate, w_down):
    bf16, f32, i32 = jnp.bfloat16, jnp.float32, jnp.int32
    rows, width = tokens.shape
    n_side, n_grp = lax.axis_size("side"), lax.axis_size("grp")
    n_x, n_z = lax.axis_size("x"), lax.axis_size("z")
    n_dev = n_x * n_z
    side = lax.axis_index("side")
    dev = lax.axis_index("x") * n_z + lax.axis_index("z")
    unit = w_gate.shape[2]

    own_gate, own_down = w_gate[0], w_down[0].T
    other_down = from_other_core(own_down)

    vmem, smem = pl.BlockSpec(memory_space=pltpu.VMEM), pl.BlockSpec(memory_space=pltpu.SMEM)
    copies = pl.pallas_call(
        functools.partial(send_kernel, rows),
        out_shape=jax.ShapeDtypeStruct((n_z, rows, width + TAIL), bf16),
        in_specs=[smem, vmem, vmem, vmem],
        out_specs=vmem,
    )(dev.reshape(1).astype(i32), tokens, expert_ids, route_weights)
    by_z = lax.all_to_all(copies, "z", split_axis=0, concat_axis=0, tiled=True).reshape(n_z * rows, -1)
    packed = lax.all_gather(by_z, "x", axis=0, tiled=True)

    group = n_dev * rows
    hit = jnp.any(packed[:, width : width + TOPK].astype(i32) == dev, axis=1)
    before = jnp.arange(group)[:, None] < jnp.arange(group)[None, :]
    slot = jnp.sum((before & hit[:, None]).astype(i32), axis=0)
    placed = (slot[None, :] == jnp.arange(CAP, dtype=i32)[:, None]) & hit[None, :]
    slot_input = jnp.dot(placed.astype(bf16), packed, preferred_element_type=f32).astype(bf16)

    def silu_gate(parts):
        block = jnp.concatenate(parts, axis=0)
        return jax.nn.silu(jnp.dot(block, gate_slab, preferred_element_type=f32)).astype(bf16)

    up = [(i, (i + 1) % n_grp) for i in range(n_grp)]
    down = [(i, (i - 1) % n_grp) for i in range(n_grp)]
    half, far = CAP // 2, n_grp // 2
    below = above = slot_input
    blocks, order, waiting, hidden = {0: slot_input}, [0], [slot_input], []
    for step in range(1, far):
        below = lax.ppermute(below, "grp", up)
        above = lax.ppermute(above, "grp", down)
        if step == 1:
            below, own_gate = lax.optimization_barrier((below, own_gate))
            other_gate = from_other_core(own_gate)
            both = [jnp.where(side == 0, own_gate, other_gate), jnp.where(side == 0, other_gate, own_gate)]
            gate_slab = jnp.pad(jnp.concatenate(both, axis=1), ((0, TAIL), (0, 0)))
        if step == far - 1:
            product = silu_gate(waiting)
            below, product = lax.optimization_barrier((below, product))
            hidden.append(product)
            waiting = []
        blocks[n_grp - step], blocks[step] = below, above
        order += [n_grp - step, step]
        waiting += [below, above]
    below, above = lax.ppermute(below[:half], "grp", up), lax.ppermute(above[half:], "grp", down)
    product = silu_gate(waiting)
    below, product = lax.optimization_barrier((below, product))
    blocks[far] = jnp.concatenate([below, above], axis=0)
    order.append(far)
    hidden += [product, silu_gate([blocks[far]])]
    hidden = jnp.concatenate(hidden, axis=0)
    got = lax.all_to_all(
        jnp.broadcast_to(hidden[None], (n_grp,) + hidden.shape), "grp", split_axis=0, concat_axis=0, tiled=True
    )

    slots = n_grp * CAP
    columns = n_side * own_down.shape[0]
    weighted = pl.pallas_call(
        functools.partial(down_kernel, n_grp, n_side, unit, rows, order),
        out_shape=jax.ShapeDtypeStruct((n_grp * group, columns), bf16),
        in_specs=[smem] + [vmem] * (3 + n_grp),
        out_specs=vmem,
        scratch_shapes=[
            pltpu.VMEM((slots, own_down.shape[1]), bf16),
            pltpu.VMEM((slots, TAIL), bf16),
        ],
        compiler_params=pltpu.CompilerParams(vmem_limit_bytes=16 * 2**20),
    )(
        jnp.stack([lax.axis_index("grp"), dev, side]).astype(i32),
        own_down,
        other_down,
        got,
        *[blocks[d][:, width:] for d in range(n_grp)],
    )
    parts = lax.all_to_all(
        weighted.reshape(n_dev * n_grp, rows, -1), ("x", "z", "grp"), split_axis=0, concat_axis=0, tiled=True
    )
    total = jnp.sum(parts.reshape(n_dev, n_grp, rows, -1).astype(f32), axis=0).astype(bf16)
    mixed = total.reshape(n_grp, rows, n_side, -1).transpose(1, 2, 0, 3)
    return mixed.reshape(rows, width)


def solution(mesh):
    side, grp, dev = mesh.devices.shape
    n_z = 8
    fine = Mesh(mesh.devices.reshape(side, grp, dev // n_z, n_z), ("side", "grp", "x", "z"))
    row_axes = ("side", "grp", "x", "z")
    in_specs = (
        P(row_axes, None),
        P(row_axes, None),
        P(row_axes, None),
        P(("x", "z"), None, ("side", "grp")),
        P(("x", "z"), None, ("side", "grp")),
    )
    return jax.shard_map(
        on_device, mesh=fine, in_specs=in_specs, out_specs=P(row_axes, None), check_vma=False
    )
```

```python
import functools

import jax
import jax.numpy as jnp
from jax import lax
from jax.experimental import pallas as pl
from jax.experimental.pallas import tpu as pltpu
from jax.sharding import Mesh, PartitionSpec as P

CAP = 32
TOPK = 8
TAIL = 128
SHIFT = 64
SPOT = 32


def send_kernel(rows, dev_ref, tokens_ref, ids_ref, weights_ref, out_ref):
    values = tokens_ref[...].astype(jnp.float32)
    width = values.shape[1]
    scale = lax.rsqrt(jnp.mean(values * values, axis=1, keepdims=True) + 1e-06)
    normed = (values * scale).astype(jnp.bfloat16)
    ids, weights = ids_ref[...].astype(jnp.float32), weights_ref[...].astype(jnp.float32)
    lane = lax.broadcasted_iota(jnp.int32, (rows, TAIL), 1)
    place = (dev_ref[0] * rows + lax.broadcasted_iota(jnp.int32, (rows, TAIL), 0)).astype(jnp.float32)
    tail = jnp.where(lane == SPOT, place, 0.0)
    for k in range(TOPK):
        tail = jnp.where(lane == k, ids[:, k : k + 1], tail)
        tail = jnp.where(lane == SHIFT + k, weights[:, k : k + 1], tail)
    tail = tail.astype(jnp.bfloat16)
    for d in range(out_ref.shape[0]):
        out_ref[d, :, :width] = normed
        out_ref[d, :, width:] = tail


def from_other_core(own):
    return lax.ppermute(own, "side", [(0, 1), (1, 0)])


def down_kernel(n_grp, n_side, unit, rows, order, where_ref, own_ref, other_ref, got_ref, *refs):
    *tails, out_ref, hidden_ref, notes_ref = refs
    grp, dev, side = where_ref[0], where_ref[1], where_ref[2]
    for g in range(n_grp):
        for j in range(n_grp):
            start = order.index((j - g) % n_grp) * CAP
            for k in range(n_side):
                at = (k * n_grp + g) * unit
                hidden_ref[j * CAP : (j + 1) * CAP, at : at + unit] = got_ref[
                    g, start : start + CAP, k * unit : (k + 1) * unit
                ]
    for d in range(n_grp):
        j = lax.rem(grp + d, n_grp)
        notes_ref[pl.ds(pl.multiple_of(j * CAP, CAP), CAP), :] = tails[d][...]
    own, other = [
        lax.dot_general(
            hidden_ref[...], slab[...], (((1,), (1,)), ((), ())), preferred_element_type=jnp.float32
        )
        for slab in (own_ref, other_ref)
    ]
    columns = [jnp.where(side == 0, own, other), jnp.where(side == 0, other, own)]
    slots, tokens = hidden_ref.shape[0], out_ref.shape[0]
    notes = notes_ref[...].astype(jnp.float32)
    lane = lax.broadcasted_iota(jnp.int32, notes.shape, 1)
    mine = (lane < TOPK) & (notes.astype(jnp.int32) == dev)
    weight = jnp.sum(jnp.where(mine, pltpu.roll(notes, SHIFT, 1), 0.0), axis=1, keepdims=True)
    place = jnp.sum(jnp.where(lane == SPOT, notes, 0.0), axis=1, keepdims=True).astype(jnp.int32)
    shift = rows.bit_length() - 1
    of_group = lax.broadcasted_iota(jnp.int32, (slots, 1), 0) // CAP
    target = (place >> shift) * (n_grp * rows) + of_group * rows + (place & (rows - 1))
    combine = jnp.where(
        lax.broadcasted_iota(jnp.int32, (slots, tokens), 1) == target, weight, 0.0
    ).astype(jnp.bfloat16)
    width = own_ref.shape[0]
    for k in range(n_side):
        out_ref[:, k * width : (k + 1) * width] = lax.dot_general(
            combine, columns[k].astype(jnp.bfloat16), (((0,), (0,)), ((), ())), preferred_element_type=jnp.float32
        ).astype(jnp.bfloat16)


def on_device(tokens, expert_ids, route_weights, w_gate, w_down):
    bf16, f32, i32 = jnp.bfloat16, jnp.float32, jnp.int32
    rows, width = tokens.shape
    n_side, n_grp = lax.axis_size("side"), lax.axis_size("grp")
    n_x, n_z = lax.axis_size("x"), lax.axis_size("z")
    n_dev = n_x * n_z
    side = lax.axis_index("side")
    dev = lax.axis_index("x") * n_z + lax.axis_index("z")
    unit = w_gate.shape[2]

    own_gate, own_down = w_gate[0], w_down[0].T
    other_down = from_other_core(own_down)

    vmem, smem = pl.BlockSpec(memory_space=pltpu.VMEM), pl.BlockSpec(memory_space=pltpu.SMEM)
    copies = pl.pallas_call(
        functools.partial(send_kernel, rows),
        out_shape=jax.ShapeDtypeStruct((n_dev, rows, width + TAIL), bf16),
        in_specs=[smem, vmem, vmem, vmem],
        out_specs=vmem,
    )(dev.reshape(1).astype(i32), tokens, expert_ids, route_weights)
    packed = lax.all_to_all(copies, ("x", "z"), split_axis=0, concat_axis=0, tiled=True)
    packed = packed.reshape(n_dev * rows, -1)

    group = n_dev * rows
    hit = jnp.any(packed[:, width : width + TOPK].astype(i32) == dev, axis=1)
    before = jnp.arange(group)[:, None] < jnp.arange(group)[None, :]
    slot = jnp.sum((before & hit[:, None]).astype(i32), axis=0)
    placed = (slot[None, :] == jnp.arange(CAP, dtype=i32)[:, None]) & hit[None, :]
    slot_input = jnp.dot(placed.astype(bf16), packed, preferred_element_type=f32).astype(bf16)

    other_gate = from_other_core(own_gate)
    both = [jnp.where(side == 0, own_gate, other_gate), jnp.where(side == 0, other_gate, own_gate)]
    gate_slab = jnp.pad(jnp.concatenate(both, axis=1), ((0, TAIL), (0, 0)))

    def silu_gate(parts):
        block = jnp.concatenate(parts, axis=0)
        return jax.nn.silu(jnp.dot(block, gate_slab, preferred_element_type=f32)).astype(bf16)

    up = [(i, (i + 1) % n_grp) for i in range(n_grp)]
    down = [(i, (i - 1) % n_grp) for i in range(n_grp)]
    half, far = CAP // 2, n_grp // 2
    below = above = slot_input
    blocks, order, waiting = {0: slot_input}, [0], [slot_input]
    for step in range(1, far):
        below = lax.ppermute(below, "grp", up)
        above = lax.ppermute(above, "grp", down)
        blocks[n_grp - step], blocks[step] = below, above
        order += [n_grp - step, step]
        waiting += [below, above]
    below, above = lax.ppermute(below[:half], "grp", up), lax.ppermute(above[half:], "grp", down)
    product = silu_gate(waiting)
    below, above, product = lax.optimization_barrier((below, above, product))
    blocks[far] = jnp.concatenate([below, above], axis=0)
    order.append(far)
    hidden = jnp.concatenate([product, silu_gate([blocks[far]])], axis=0)
    got = lax.all_to_all(
        jnp.broadcast_to(hidden[None], (n_grp,) + hidden.shape), "grp", split_axis=0, concat_axis=0, tiled=True
    )

    slots = n_grp * CAP
    columns = n_side * own_down.shape[0]
    weighted = pl.pallas_call(
        functools.partial(down_kernel, n_grp, n_side, unit, rows, order),
        out_shape=jax.ShapeDtypeStruct((n_grp * group, columns), bf16),
        in_specs=[smem] + [vmem] * (3 + n_grp),
        out_specs=vmem,
        scratch_shapes=[
            pltpu.VMEM((slots, own_down.shape[1]), bf16),
            pltpu.VMEM((slots, TAIL), bf16),
        ],
        compiler_params=pltpu.CompilerParams(vmem_limit_bytes=16 * 2**20),
    )(
        jnp.stack([lax.axis_index("grp"), dev, side]).astype(i32),
        own_down,
        other_down,
        got,
        *[blocks[d][:, width:] for d in range(n_grp)],
    )
    parts = lax.all_to_all(
        weighted.reshape(n_dev * n_grp, rows, -1), ("x", "z", "grp"), split_axis=0, concat_axis=0, tiled=True
    )
    total = jnp.sum(parts.reshape(n_dev, n_grp, rows, -1).astype(f32), axis=0).astype(bf16)
    mixed = total.reshape(n_grp, rows, n_side, -1).transpose(1, 2, 0, 3)
    return mixed.reshape(rows, width)


def solution(mesh):
    side, grp, dev = mesh.devices.shape
    n_z = 8
    fine = Mesh(mesh.devices.reshape(side, grp, dev // n_z, n_z), ("side", "grp", "x", "z"))
    row_axes = ("side", "grp", "x", "z")
    in_specs = (
        P(row_axes, None),
        P(row_axes, None),
        P(row_axes, None),
        P(("x", "z"), None, ("side", "grp")),
        P(("x", "z"), None, ("side", "grp")),
    )
    return jax.shard_map(
        on_device, mesh=fine, in_specs=in_specs, out_specs=P(row_axes, None), check_vma=False
    )
```

```python
import functools

import jax
import jax.numpy as jnp
from jax import lax
from jax.experimental import pallas as pl
from jax.experimental.pallas import tpu as pltpu
from jax.sharding import Mesh, PartitionSpec as P

CAP = 32
TOPK = 8
TAIL = 128
SHIFT = 64
SPOT = 32


def send_kernel(rows, dev_ref, tokens_ref, ids_ref, weights_ref, out_ref):
    values = tokens_ref[...].astype(jnp.float32)
    width = values.shape[1]
    scale = lax.rsqrt(jnp.mean(values * values, axis=1, keepdims=True) + 1e-06)
    normed = (values * scale).astype(jnp.bfloat16)
    ids, weights = ids_ref[...].astype(jnp.float32), weights_ref[...].astype(jnp.float32)
    lane = lax.broadcasted_iota(jnp.int32, (rows, TAIL), 1)
    place = (dev_ref[0] * rows + lax.broadcasted_iota(jnp.int32, (rows, TAIL), 0)).astype(jnp.float32)
    tail = jnp.where(lane == SPOT, place, 0.0)
    for k in range(TOPK):
        tail = jnp.where(lane == k, ids[:, k : k + 1], tail)
        tail = jnp.where(lane == SHIFT + k, weights[:, k : k + 1], tail)
    tail = tail.astype(jnp.bfloat16)
    for d in range(out_ref.shape[0]):
        out_ref[d, :, :width] = normed
        out_ref[d, :, width:] = tail


def from_other_core(own):
    return lax.ppermute(own, "side", [(0, 1), (1, 0)])


def down_kernel(n_grp, n_side, unit, rows, order, where_ref, own_ref, other_ref, got_ref, *refs):
    *tails, out_ref, hidden_ref, notes_ref = refs
    grp, dev, side = where_ref[0], where_ref[1], where_ref[2]
    for g in range(n_grp):
        for j in range(n_grp):
            start = order.index((j - g) % n_grp) * CAP
            for k in range(n_side):
                at = (k * n_grp + g) * unit
                hidden_ref[j * CAP : (j + 1) * CAP, at : at + unit] = got_ref[
                    g, start : start + CAP, k * unit : (k + 1) * unit
                ]
    for d in range(n_grp):
        j = lax.rem(grp + d, n_grp)
        notes_ref[pl.ds(pl.multiple_of(j * CAP, CAP), CAP), :] = tails[d][...]
    own, other = [
        lax.dot_general(
            hidden_ref[...], slab[...], (((1,), (1,)), ((), ())), preferred_element_type=jnp.float32
        )
        for slab in (own_ref, other_ref)
    ]
    columns = [jnp.where(side == 0, own, other), jnp.where(side == 0, other, own)]
    slots, tokens = hidden_ref.shape[0], out_ref.shape[0]
    notes = notes_ref[...].astype(jnp.float32)
    lane = lax.broadcasted_iota(jnp.int32, notes.shape, 1)
    mine = (lane < TOPK) & (notes.astype(jnp.int32) == dev)
    weight = jnp.sum(jnp.where(mine, pltpu.roll(notes, SHIFT, 1), 0.0), axis=1, keepdims=True)
    place = jnp.sum(jnp.where(lane == SPOT, notes, 0.0), axis=1, keepdims=True).astype(jnp.int32)
    shift = rows.bit_length() - 1
    of_group = lax.broadcasted_iota(jnp.int32, (slots, 1), 0) // CAP
    target = (place >> shift) * (n_grp * rows) + of_group * rows + (place & (rows - 1))
    combine = jnp.where(
        lax.broadcasted_iota(jnp.int32, (slots, tokens), 1) == target, weight, 0.0
    ).astype(jnp.bfloat16)
    width = own_ref.shape[0]
    for k in range(n_side):
        out_ref[:, k * width : (k + 1) * width] = lax.dot_general(
            combine, columns[k].astype(jnp.bfloat16), (((0,), (0,)), ((), ())), preferred_element_type=jnp.float32
        ).astype(jnp.bfloat16)


def on_device(tokens, expert_ids, route_weights, w_gate, w_down):
    bf16, f32, i32 = jnp.bfloat16, jnp.float32, jnp.int32
    rows, width = tokens.shape
    n_side, n_grp = lax.axis_size("side"), lax.axis_size("grp")
    n_x, n_z = lax.axis_size("x"), lax.axis_size("z")
    n_dev = n_x * n_z
    side = lax.axis_index("side")
    dev = lax.axis_index("x") * n_z + lax.axis_index("z")
    unit = w_gate.shape[2]

    own_gate, own_down = w_gate[0], w_down[0].T
    other_down = from_other_core(own_down)

    vmem, smem = pl.BlockSpec(memory_space=pltpu.VMEM), pl.BlockSpec(memory_space=pltpu.SMEM)
    copies = pl.pallas_call(
        functools.partial(send_kernel, rows),
        out_shape=jax.ShapeDtypeStruct((n_dev, rows, width + TAIL), bf16),
        in_specs=[smem, vmem, vmem, vmem],
        out_specs=vmem,
    )(dev.reshape(1).astype(i32), tokens, expert_ids, route_weights)
    packed = lax.all_to_all(copies, ("x", "z"), split_axis=0, concat_axis=0, tiled=True)
    packed = packed.reshape(n_dev * rows, -1)

    group = n_dev * rows
    hit = jnp.any(packed[:, width : width + TOPK].astype(i32) == dev, axis=1)
    before = jnp.arange(group)[:, None] < jnp.arange(group)[None, :]
    slot = jnp.sum((before & hit[:, None]).astype(i32), axis=0)
    placed = (slot[None, :] == jnp.arange(CAP, dtype=i32)[:, None]) & hit[None, :]
    slot_input = jnp.dot(placed.astype(bf16), packed, preferred_element_type=f32).astype(bf16)

    other_gate = from_other_core(own_gate)
    both = [jnp.where(side == 0, own_gate, other_gate), jnp.where(side == 0, other_gate, own_gate)]
    gate_slab = jnp.pad(jnp.concatenate(both, axis=1), ((0, TAIL), (0, 0)))

    def silu_gate(parts):
        block = jnp.concatenate(parts, axis=0)
        return jax.nn.silu(jnp.dot(block, gate_slab, preferred_element_type=f32)).astype(bf16)

    up = [(i, (i + 1) % n_grp) for i in range(n_grp)]
    down = [(i, (i - 1) % n_grp) for i in range(n_grp)]
    half, far = CAP // 2, n_grp // 2
    below = above = slot_input
    blocks, order, waiting = {0: slot_input}, [0], [slot_input]
    for step in range(1, far):
        below = lax.ppermute(below, "grp", up)
        above = lax.ppermute(above, "grp", down)
        blocks[n_grp - step], blocks[step] = below, above
        order += [n_grp - step, step]
        waiting += [below, above]
    below, above = lax.ppermute(below[:half], "grp", up), lax.ppermute(above[half:], "grp", down)
    product = silu_gate(waiting)
    below, above, product = lax.optimization_barrier((below, above, product))
    blocks[far] = jnp.concatenate([below, above], axis=0)
    order.append(far)
    hidden = jnp.concatenate([product, silu_gate([blocks[far]])], axis=0)
    got = lax.all_to_all(
        jnp.broadcast_to(hidden[None], (n_grp,) + hidden.shape), "grp", split_axis=0, concat_axis=0, tiled=True
    )

    slots = n_grp * CAP
    columns = n_side * own_down.shape[0]
    weighted = pl.pallas_call(
        functools.partial(down_kernel, n_grp, n_side, unit, rows, order),
        out_shape=jax.ShapeDtypeStruct((n_grp * group, columns), bf16),
        in_specs=[smem] + [vmem] * (3 + n_grp),
        out_specs=vmem,
        scratch_shapes=[
            pltpu.VMEM((slots, own_down.shape[1]), bf16),
            pltpu.VMEM((slots, TAIL), bf16),
        ],
        compiler_params=pltpu.CompilerParams(vmem_limit_bytes=16 * 2**20),
    )(
        jnp.stack([lax.axis_index("grp"), dev, side]).astype(i32),
        own_down,
        other_down,
        got,
        *[blocks[d][:, width:] for d in range(n_grp)],
    )
    over_x = lax.all_to_all(
        weighted.reshape(n_x, n_z * n_grp * rows, -1), "x", split_axis=0, concat_axis=0, tiled=True
    )
    total_x = jnp.sum(over_x.astype(f32), axis=0).astype(bf16)
    parts = lax.all_to_all(
        total_x.reshape(n_z * n_grp, rows, -1), ("z", "grp"), split_axis=0, concat_axis=0, tiled=True
    )
    total = jnp.sum(parts.reshape(n_z, n_grp, rows, -1).astype(f32), axis=0).astype(bf16)
    mixed = total.reshape(n_grp, rows, n_side, -1).transpose(1, 2, 0, 3)
    return mixed.reshape(rows, width)


def solution(mesh):
    side, grp, dev = mesh.devices.shape
    n_z = 8
    fine = Mesh(mesh.devices.reshape(side, grp, dev // n_z, n_z), ("side", "grp", "x", "z"))
    row_axes = ("side", "grp", "x", "z")
    in_specs = (
        P(row_axes, None),
        P(row_axes, None),
        P(row_axes, None),
        P(("x", "z"), None, ("side", "grp")),
        P(("x", "z"), None, ("side", "grp")),
    )
    return jax.shard_map(
        on_device, mesh=fine, in_specs=in_specs, out_specs=P(row_axes, None), check_vma=False
    )
```

```python
import functools

import jax
import jax.numpy as jnp
from jax import lax
from jax.experimental import pallas as pl
from jax.experimental.pallas import tpu as pltpu
from jax.sharding import Mesh, PartitionSpec as P

CAP = 32
TOPK = 8
TAIL = 128
SHIFT = 64
SPOT = 32


def send_kernel(rows, dev_ref, tokens_ref, ids_ref, weights_ref, out_ref):
    values = tokens_ref[...].astype(jnp.float32)
    width = values.shape[1]
    scale = lax.rsqrt(jnp.mean(values * values, axis=1, keepdims=True) + 1e-06)
    normed = (values * scale).astype(jnp.bfloat16)
    ids, weights = ids_ref[...].astype(jnp.float32), weights_ref[...].astype(jnp.float32)
    lane = lax.broadcasted_iota(jnp.int32, (rows, TAIL), 1)
    place = (dev_ref[0] * rows + lax.broadcasted_iota(jnp.int32, (rows, TAIL), 0)).astype(jnp.float32)
    tail = jnp.where(lane == SPOT, place, 0.0)
    for k in range(TOPK):
        tail = jnp.where(lane == k, ids[:, k : k + 1], tail)
        tail = jnp.where(lane == SHIFT + k, weights[:, k : k + 1], tail)
    tail = tail.astype(jnp.bfloat16)
    for d in range(out_ref.shape[0]):
        out_ref[d, :, :width] = normed
        out_ref[d, :, width:] = tail


def from_other_core(own):
    return lax.ppermute(own, "side", [(0, 1), (1, 0)])


def down_kernel(n_grp, n_side, unit, rows, order, where_ref, own_ref, other_ref, got_ref, *refs):
    *tails, out_ref, hidden_ref, notes_ref = refs
    grp, dev, side = where_ref[0], where_ref[1], where_ref[2]
    for g in range(n_grp):
        for j in range(n_grp):
            start = order.index((j - g) % n_grp) * CAP
            for k in range(n_side):
                at = (k * n_grp + g) * unit
                hidden_ref[j * CAP : (j + 1) * CAP, at : at + unit] = got_ref[
                    g, start : start + CAP, k * unit : (k + 1) * unit
                ]
    for d in range(n_grp):
        j = lax.rem(grp + d, n_grp)
        notes_ref[pl.ds(pl.multiple_of(j * CAP, CAP), CAP), :] = tails[d][...]
    own, other = [
        lax.dot_general(
            hidden_ref[...], slab[...], (((1,), (1,)), ((), ())), preferred_element_type=jnp.float32
        )
        for slab in (own_ref, other_ref)
    ]
    columns = [jnp.where(side == 0, own, other), jnp.where(side == 0, other, own)]
    slots, tokens = hidden_ref.shape[0], out_ref.shape[0]
    notes = notes_ref[...].astype(jnp.float32)
    lane = lax.broadcasted_iota(jnp.int32, notes.shape, 1)
    mine = (lane < TOPK) & (notes.astype(jnp.int32) == dev)
    weight = jnp.sum(jnp.where(mine, pltpu.roll(notes, SHIFT, 1), 0.0), axis=1, keepdims=True)
    place = jnp.sum(jnp.where(lane == SPOT, notes, 0.0), axis=1, keepdims=True).astype(jnp.int32)
    shift = rows.bit_length() - 1
    of_group = lax.broadcasted_iota(jnp.int32, (slots, 1), 0) // CAP
    target = (place >> shift) * (n_grp * rows) + of_group * rows + (place & (rows - 1))
    combine = jnp.where(
        lax.broadcasted_iota(jnp.int32, (slots, tokens), 1) == target, weight, 0.0
    ).astype(jnp.bfloat16)
    width = own_ref.shape[0]
    for k in range(n_side):
        out_ref[:, k * width : (k + 1) * width] = lax.dot_general(
            combine, columns[k].astype(jnp.bfloat16), (((0,), (0,)), ((), ())), preferred_element_type=jnp.float32
        ).astype(jnp.bfloat16)


def on_device(tokens, expert_ids, route_weights, w_gate, w_down):
    bf16, f32, i32 = jnp.bfloat16, jnp.float32, jnp.int32
    rows, width = tokens.shape
    n_side, n_grp = lax.axis_size("side"), lax.axis_size("grp")
    n_x, n_z = lax.axis_size("x"), lax.axis_size("z")
    n_dev = n_x * n_z
    side = lax.axis_index("side")
    dev = lax.axis_index("x") * n_z + lax.axis_index("z")
    unit = w_gate.shape[2]

    own_gate, own_down = w_gate[0], w_down[0].T
    other_gate = from_other_core(own_gate)

    vmem, smem = pl.BlockSpec(memory_space=pltpu.VMEM), pl.BlockSpec(memory_space=pltpu.SMEM)
    copies = pl.pallas_call(
        functools.partial(send_kernel, rows),
        out_shape=jax.ShapeDtypeStruct((n_z, rows, width + TAIL), bf16),
        in_specs=[smem, vmem, vmem, vmem],
        out_specs=vmem,
    )(dev.reshape(1).astype(i32), tokens, expert_ids, route_weights)
    by_z = lax.all_to_all(copies, "z", split_axis=0, concat_axis=0, tiled=True).reshape(n_z * rows, -1)
    by_z, other_gate = lax.optimization_barrier((by_z, other_gate))
    packed = lax.all_gather(by_z, "x", axis=0, tiled=True)

    group = n_dev * rows
    hit = jnp.any(packed[:, width : width + TOPK].astype(i32) == dev, axis=1)
    before = jnp.arange(group)[:, None] < jnp.arange(group)[None, :]
    slot = jnp.sum((before & hit[:, None]).astype(i32), axis=0)
    placed = (slot[None, :] == jnp.arange(CAP, dtype=i32)[:, None]) & hit[None, :]
    slot_input = jnp.dot(placed.astype(bf16), packed, preferred_element_type=f32).astype(bf16)

    both = [jnp.where(side == 0, own_gate, other_gate), jnp.where(side == 0, other_gate, own_gate)]
    gate_slab = jnp.pad(jnp.concatenate(both, axis=1), ((0, TAIL), (0, 0)))

    def silu_gate(parts):
        block = jnp.concatenate(parts, axis=0)
        return jax.nn.silu(jnp.dot(block, gate_slab, preferred_element_type=f32)).astype(bf16)

    up = [(i, (i + 1) % n_grp) for i in range(n_grp)]
    down = [(i, (i - 1) % n_grp) for i in range(n_grp)]
    half, far = CAP // 2, n_grp // 2
    below = above = slot_input
    blocks, order, waiting = {0: slot_input}, [0], [slot_input]
    for step in range(1, far):
        below = lax.ppermute(below, "grp", up)
        above = lax.ppermute(above, "grp", down)
        blocks[n_grp - step], blocks[step] = below, above
        order += [n_grp - step, step]
        waiting += [below, above]
    below, above = lax.ppermute(below[:half], "grp", up), lax.ppermute(above[half:], "grp", down)
    product = silu_gate(waiting)
    below, above, product = lax.optimization_barrier((below, above, product))
    blocks[far] = jnp.concatenate([below, above], axis=0)
    order.append(far)
    hidden = jnp.concatenate([product, silu_gate([blocks[far]])], axis=0)
    hidden, own_down = lax.optimization_barrier((hidden, own_down))
    other_down = from_other_core(own_down)
    got = lax.all_to_all(
        jnp.broadcast_to(hidden[None], (n_grp,) + hidden.shape), "grp", split_axis=0, concat_axis=0, tiled=True
    )

    slots = n_grp * CAP
    columns = n_side * own_down.shape[0]
    weighted = pl.pallas_call(
        functools.partial(down_kernel, n_grp, n_side, unit, rows, order),
        out_shape=jax.ShapeDtypeStruct((n_grp * group, columns), bf16),
        in_specs=[smem] + [vmem] * (3 + n_grp),
        out_specs=vmem,
        scratch_shapes=[
            pltpu.VMEM((slots, own_down.shape[1]), bf16),
            pltpu.VMEM((slots, TAIL), bf16),
        ],
        compiler_params=pltpu.CompilerParams(vmem_limit_bytes=16 * 2**20),
    )(
        jnp.stack([lax.axis_index("grp"), dev, side]).astype(i32),
        own_down,
        other_down,
        got,
        *[blocks[d][:, width:] for d in range(n_grp)],
    )
    over_x = lax.all_to_all(
        weighted.reshape(n_x, n_z * n_grp * rows, -1), "x", split_axis=0, concat_axis=0, tiled=True
    )
    total_x = jnp.sum(over_x.astype(f32), axis=0).astype(bf16)
    parts = lax.all_to_all(
        total_x.reshape(n_z * n_grp, rows, -1), ("z", "grp"), split_axis=0, concat_axis=0, tiled=True
    )
    total = jnp.sum(parts.reshape(n_z, n_grp, rows, -1).astype(f32), axis=0).astype(bf16)
    mixed = total.reshape(n_grp, rows, n_side, -1).transpose(1, 2, 0, 3)
    return mixed.reshape(rows, width)


def solution(mesh):
    side, grp, dev = mesh.devices.shape
    n_z = 8
    fine = Mesh(mesh.devices.reshape(side, grp, dev // n_z, n_z), ("side", "grp", "x", "z"))
    row_axes = ("side", "grp", "x", "z")
    in_specs = (
        P(row_axes, None),
        P(row_axes, None),
        P(row_axes, None),
        P(("x", "z"), None, ("side", "grp")),
        P(("x", "z"), None, ("side", "grp")),
    )
    return jax.shard_map(
        on_device, mesh=fine, in_specs=in_specs, out_specs=P(row_axes, None), check_vma=False
    )
```

```python
import functools

import jax
import jax.numpy as jnp
from jax import lax
from jax.experimental import pallas as pl
from jax.experimental.pallas import tpu as pltpu
from jax.sharding import Mesh, PartitionSpec as P

CAP = 32
TOPK = 8
TAIL = 128
SHIFT = 64
SPOT = 32


def send_kernel(rows, dev_ref, tokens_ref, ids_ref, weights_ref, out_ref):
    values = tokens_ref[...].astype(jnp.float32)
    width = values.shape[1]
    scale = lax.rsqrt(jnp.mean(values * values, axis=1, keepdims=True) + 1e-06)
    normed = (values * scale).astype(jnp.bfloat16)
    ids, weights = ids_ref[...].astype(jnp.float32), weights_ref[...].astype(jnp.float32)
    lane = lax.broadcasted_iota(jnp.int32, (rows, TAIL), 1)
    place = (dev_ref[0] * rows + lax.broadcasted_iota(jnp.int32, (rows, TAIL), 0)).astype(jnp.float32)
    tail = jnp.where(lane == SPOT, place, 0.0)
    for k in range(TOPK):
        tail = jnp.where(lane == k, ids[:, k : k + 1], tail)
        tail = jnp.where(lane == SHIFT + k, weights[:, k : k + 1], tail)
    tail = tail.astype(jnp.bfloat16)
    for d in range(out_ref.shape[0]):
        out_ref[d, :, :width] = normed
        out_ref[d, :, width:] = tail


def from_other_core(own):
    return lax.ppermute(own, "side", [(0, 1), (1, 0)])


def hidden_kernel(first_ref, second_ref, near_ref, slab_ref, out_ref):
    block = jnp.concatenate([first_ref[...], second_ref[...]], axis=0)
    gate = jnp.dot(block, slab_ref[...], preferred_element_type=jnp.float32)
    far = jax.nn.silu(gate).astype(jnp.bfloat16)
    near = near_ref[...]
    for g in range(out_ref.shape[0]):
        out_ref[g, : near.shape[0]] = near
        out_ref[g, near.shape[0] :] = far


def down_kernel(n_grp, n_side, unit, rows, order, where_ref, own_ref, other_ref, got_ref, *refs):
    *tails, out_ref, hidden_ref, notes_ref = refs
    grp, dev, side = where_ref[0], where_ref[1], where_ref[2]
    for g in range(n_grp):
        for j in range(n_grp):
            start = order.index((j - g) % n_grp) * CAP
            for k in range(n_side):
                at = (k * n_grp + g) * unit
                hidden_ref[j * CAP : (j + 1) * CAP, at : at + unit] = got_ref[
                    g, start : start + CAP, k * unit : (k + 1) * unit
                ]
    for d in range(n_grp):
        j = lax.rem(grp + d, n_grp)
        notes_ref[pl.ds(pl.multiple_of(j * CAP, CAP), CAP), :] = tails[d][...]
    own, other = [
        lax.dot_general(
            hidden_ref[...], slab[...], (((1,), (1,)), ((), ())), preferred_element_type=jnp.float32
        )
        for slab in (own_ref, other_ref)
    ]
    columns = [jnp.where(side == 0, own, other), jnp.where(side == 0, other, own)]
    slots, tokens = hidden_ref.shape[0], out_ref.shape[0]
    notes = notes_ref[...].astype(jnp.float32)
    lane = lax.broadcasted_iota(jnp.int32, notes.shape, 1)
    mine = (lane < TOPK) & (notes.astype(jnp.int32) == dev)
    weight = jnp.sum(jnp.where(mine, pltpu.roll(notes, SHIFT, 1), 0.0), axis=1, keepdims=True)
    place = jnp.sum(jnp.where(lane == SPOT, notes, 0.0), axis=1, keepdims=True).astype(jnp.int32)
    shift = rows.bit_length() - 1
    of_group = lax.broadcasted_iota(jnp.int32, (slots, 1), 0) // CAP
    target = (place >> shift) * (n_grp * rows) + of_group * rows + (place & (rows - 1))
    combine = jnp.where(
        lax.broadcasted_iota(jnp.int32, (slots, tokens), 1) == target, weight, 0.0
    ).astype(jnp.bfloat16)
    width = own_ref.shape[0]
    for k in range(n_side):
        out_ref[:, k * width : (k + 1) * width] = lax.dot_general(
            combine, columns[k].astype(jnp.bfloat16), (((0,), (0,)), ((), ())), preferred_element_type=jnp.float32
        ).astype(jnp.bfloat16)


def on_device(tokens, expert_ids, route_weights, w_gate, w_down):
    bf16, f32, i32 = jnp.bfloat16, jnp.float32, jnp.int32
    rows, width = tokens.shape
    n_side, n_grp = lax.axis_size("side"), lax.axis_size("grp")
    n_x, n_z = lax.axis_size("x"), lax.axis_size("z")
    n_dev = n_x * n_z
    side = lax.axis_index("side")
    dev = lax.axis_index("x") * n_z + lax.axis_index("z")
    unit = w_gate.shape[2]

    own_gate, own_down = w_gate[0], w_down[0].T
    other_gate = from_other_core(own_gate)

    vmem, smem = pl.BlockSpec(memory_space=pltpu.VMEM), pl.BlockSpec(memory_space=pltpu.SMEM)
    copies = pl.pallas_call(
        functools.partial(send_kernel, rows),
        out_shape=jax.ShapeDtypeStruct((n_z, rows, width + TAIL), bf16),
        in_specs=[smem, vmem, vmem, vmem],
        out_specs=vmem,
    )(dev.reshape(1).astype(i32), tokens, expert_ids, route_weights)
    by_z = lax.all_to_all(copies, "z", split_axis=0, concat_axis=0, tiled=True).reshape(n_z * rows, -1)
    by_z, other_gate = lax.optimization_barrier((by_z, other_gate))
    packed = lax.all_gather(by_z, "x", axis=0, tiled=True)

    group = n_dev * rows
    hit = jnp.any(packed[:, width : width + TOPK].astype(i32) == dev, axis=1)
    before = jnp.arange(group)[:, None] < jnp.arange(group)[None, :]
    slot = jnp.sum((before & hit[:, None]).astype(i32), axis=0)
    placed = (slot[None, :] == jnp.arange(CAP, dtype=i32)[:, None]) & hit[None, :]
    slot_input = jnp.dot(placed.astype(bf16), packed, preferred_element_type=f32).astype(bf16)

    both = [jnp.where(side == 0, own_gate, other_gate), jnp.where(side == 0, other_gate, own_gate)]
    gate_slab = jnp.pad(jnp.concatenate(both, axis=1), ((0, TAIL), (0, 0)))

    def silu_gate(parts):
        block = jnp.concatenate(parts, axis=0)
        return jax.nn.silu(jnp.dot(block, gate_slab, preferred_element_type=f32)).astype(bf16)

    up = [(i, (i + 1) % n_grp) for i in range(n_grp)]
    down = [(i, (i - 1) % n_grp) for i in range(n_grp)]
    half, far = CAP // 2, n_grp // 2
    below = above = slot_input
    blocks, order, waiting = {0: slot_input}, [0], [slot_input]
    for step in range(1, far):
        below = lax.ppermute(below, "grp", up)
        above = lax.ppermute(above, "grp", down)
        blocks[n_grp - step], blocks[step] = below, above
        order += [n_grp - step, step]
        waiting += [below, above]
    below, above = lax.ppermute(below[:half], "grp", up), lax.ppermute(above[half:], "grp", down)
    product = silu_gate(waiting)
    below, above, product = lax.optimization_barrier((below, above, product))
    blocks[far] = jnp.concatenate([below, above], axis=0)
    order.append(far)
    hidden = pl.pallas_call(
        hidden_kernel,
        out_shape=jax.ShapeDtypeStruct((n_grp, n_grp * CAP, n_side * unit), bf16),
        in_specs=[vmem] * 4,
        out_specs=vmem,
        compiler_params=pltpu.CompilerParams(vmem_limit_bytes=16 * 2**20),
    )(below, above, product, gate_slab)
    hidden, own_down = lax.optimization_barrier((hidden, own_down))
    other_down = from_other_core(own_down)
    got = lax.all_to_all(hidden, "grp", split_axis=0, concat_axis=0, tiled=True)

    slots = n_grp * CAP
    columns = n_side * own_down.shape[0]
    weighted = pl.pallas_call(
        functools.partial(down_kernel, n_grp, n_side, unit, rows, order),
        out_shape=jax.ShapeDtypeStruct((n_grp * group, columns), bf16),
        in_specs=[smem] + [vmem] * (3 + n_grp),
        out_specs=vmem,
        scratch_shapes=[
            pltpu.VMEM((slots, own_down.shape[1]), bf16),
            pltpu.VMEM((slots, TAIL), bf16),
        ],
        compiler_params=pltpu.CompilerParams(vmem_limit_bytes=16 * 2**20),
    )(
        jnp.stack([lax.axis_index("grp"), dev, side]).astype(i32),
        own_down,
        other_down,
        got,
        *[blocks[d][:, width:] for d in range(n_grp)],
    )
    over_x = lax.all_to_all(
        weighted.reshape(n_x, n_z * n_grp * rows, -1), "x", split_axis=0, concat_axis=0, tiled=True
    )
    total_x = jnp.sum(over_x.astype(f32), axis=0).astype(bf16)
    parts = lax.all_to_all(
        total_x.reshape(n_z * n_grp, rows, -1), ("z", "grp"), split_axis=0, concat_axis=0, tiled=True
    )
    total = jnp.sum(parts.reshape(n_z, n_grp, rows, -1).astype(f32), axis=0).astype(bf16)
    mixed = total.reshape(n_grp, rows, n_side, -1).transpose(1, 2, 0, 3)
    return mixed.reshape(rows, width)


def solution(mesh):
    side, grp, dev = mesh.devices.shape
    n_z = 8
    fine = Mesh(mesh.devices.reshape(side, grp, dev // n_z, n_z), ("side", "grp", "x", "z"))
    row_axes = ("side", "grp", "x", "z")
    in_specs = (
        P(row_axes, None),
        P(row_axes, None),
        P(row_axes, None),
        P(("x", "z"), None, ("side", "grp")),
        P(("x", "z"), None, ("side", "grp")),
    )
    return jax.shard_map(
        on_device, mesh=fine, in_specs=in_specs, out_specs=P(row_axes, None), check_vma=False
    )
```
